32 devices in a mesh: group: 2 (over core), shard: 16 (over z, y, x).
Axes of the slice: x: 2, y: 2, z: 4, core: 2. Of those that a mesh axis runs over, the one named last changes fastest.
Arguments:
- latents: bfloat16 [64, 32, 32, 320], P(('group', 'shard')), may hold values from -6 to 6
- cotangent: bfloat16 [64, 32, 32, 320], P(('group', 'shard')), may hold values from -6 to 6
- weights: float32 [2, 2880, 320], P('group', 'shard'), may hold values from -0.109375 to 0.109375
- momentum: float32 [2, 2880, 320], P('group', 'shard'), may hold values from -6 to 6
- step: int32 [1], replicated, may hold values from 0 to 63
Outputs:
- activations: float32 [64, 32, 32, 320], P(('group', 'shard'))
- data_grad: float32 [64, 32, 32, 320], P(('group', 'shard'))
- new_weights: float32 [2, 2880, 320], P('group', 'shard')
- new_momentum: float32 [2, 2880, 320], P('group', 'shard')
The draws below stay inside these ranges and needn't reach their ends.
Inputs may be any that keep to these rules, and one draw needn't show every extreme that they name: `step`: one value shared by all devices.
All inputs are finite; a program needn't handle non-finite values.
Results may differ from the reference program's by a relative error of at most 0.0029.
Values may be sent and summed in bfloat16 or wider, within the bound.
A program may use at most 128 MiB of HBM per device.

```python
import jax
import jax.numpy as jnp
from jax import lax

C = 320
IMG_DEV = 2
HH = 32
WW = 32
IMAGES = 64
KROWS = 2880
N_GROUP = 2
N_SHARD = 16


def steps_of(stream_key, extent, pieces, least, largest):
    loudness, own = 1.0, jax.random.fold_in(stream_key, 6)
    for position, shards_of in pieces:
        steps = jnp.exp(jax.random.uniform(jax.random.fold_in(own, position), (shards_of,), jnp.float32, least / len(pieces), largest / len(pieces)))
        loudness = loudness * jnp.repeat(steps, extent[position] // shards_of).reshape([-1 if axis == position else 1 for axis in range(len(extent))])
    return loudness


def scatter_about(stream_key, extent, deviation, most, split=(), held_as=jnp.bfloat16):
    array = jax.random.normal(stream_key, extent, jnp.float32) * deviation
    if len(split) > 0:
        array = steps_of(stream_key, extent, split, -0.22, 0.18) * array
    return jnp.clip(array, min=-most, max=most).astype(held_as)


def setup_inputs(seed: int = 0) -> dict:
    seeds = jax.random.split(jax.random.key(seed), 6)
    latents = scatter_about(seeds[0], (IMAGES, HH, WW, C), 1.0, 6.0, ((0, 32),))
    cotangent = scatter_about(seeds[1], (IMAGES, HH, WW, C), 1.0, 6.0, ((0, 32),))
    weights = scatter_about(seeds[2], (N_GROUP, KROWS, C), (9 * C) ** -0.5, 0.109375, ((0, 2), (1, 16)), jnp.float32)
    momentum = scatter_about(seeds[3], (N_GROUP, KROWS, C), 1.0, 6.0, ((0, 2), (1, 16)), jnp.float32)
    step = jax.random.randint(seeds[4], (1,), 0, 64).astype(jnp.int32)
    return dict(latents=latents, cotangent=cotangent, weights=weights, momentum=momentum, step=step)


beta_rate = 0.9
peak_rate = 0.1
warm_steps = 64.0
tap_offsets = [(row_off, col_off) for row_off in (-1, 0, 1) for col_off in (-1, 0, 1)]


def shifted_view(padded, row_off, col_off):
    height = padded.shape[1] - 2
    width = padded.shape[2] - 2
    return padded[:, 1 + row_off:1 + row_off + height, 1 + col_off:1 + col_off + width, :]


def conv_step(latents, cotangent, kernel):
    channels = kernel.shape[1]
    image_shape = latents.shape
    cell_count = image_shape[0] * image_shape[1] * image_shape[2]
    pad_in = jnp.pad(latents, ((0, 0), (1, 1), (1, 1), (0, 0)))
    pad_co = jnp.pad(cotangent, ((0, 0), (1, 1), (1, 1), (0, 0)))
    flat_co = cotangent.reshape(cell_count, channels)
    forward = jnp.zeros((cell_count, channels), jnp.float32)
    backward = jnp.zeros((cell_count, channels), jnp.float32)
    tap_grads = []
    for tap_index, (row_off, col_off) in enumerate(tap_offsets):
        tap_kernel = kernel[tap_index * channels:(tap_index + 1) * channels]
        moved_in = shifted_view(pad_in, row_off, col_off).reshape(cell_count, channels)
        moved_co = shifted_view(pad_co, -row_off, -col_off).reshape(cell_count, channels)
        forward = forward + jnp.dot(moved_in, tap_kernel, preferred_element_type=jnp.float32)
        backward = backward + lax.dot_general(moved_co, tap_kernel, (((1,), (1,)), ((), ())), preferred_element_type=jnp.float32)
        tap_grads.append(lax.dot_general(moved_in, flat_co, (((0,), (0,)), ((), ())), preferred_element_type=jnp.float32))
    return (forward.reshape(image_shape),
            backward.reshape(image_shape),
            jnp.concatenate(tap_grads, 0))


def reference(latents, cotangent, weights, momentum, step):
    per_group = latents.shape[0] // N_GROUP
    grad_scale = float(N_SHARD * IMG_DEV * HH * WW) ** -0.5
    learn_rate = peak_rate * (step[0] + 1).astype(jnp.float32) / warm_steps
    acts_list = []
    back_list = []
    updated_list = []
    moment_list = []
    for group in range(N_GROUP):
        kernel = weights[group].astype(jnp.bfloat16)
        first = group * per_group

        def one_image(total, images):
            forward_img, backward_img, term = conv_step(images[0][None], images[1][None], kernel)
            return total + term, (forward_img[0], backward_img[0])

        total, outputs = lax.scan(one_image, jnp.zeros(kernel.shape, jnp.float32),
                                  (latents[first:first + per_group], cotangent[first:first + per_group]))
        acts_list.append(outputs[0])
        back_list.append(outputs[1])
        moment = beta_rate * momentum[group] + total * grad_scale
        moment_list.append(moment)
        updated_list.append(weights[group] - learn_rate * moment)
    updated = jnp.stack(updated_list, 0)
    moments = jnp.stack(moment_list, 0)
    bit_count = N_GROUP.bit_length() - 1
    distance = step[0] % bit_count
    partner = jnp.bitwise_xor(jnp.arange(N_GROUP, dtype=jnp.int32), jnp.left_shift(jnp.int32(1), distance.astype(jnp.int32)))
    new_weights = 0.5 * (updated + jnp.take(updated, partner, axis=0))
    new_momentum = 0.5 * (moments + jnp.take(moments, partner, axis=0))
    return (jnp.concatenate(acts_list, 0), jnp.concatenate(back_list, 0), new_weights, new_momentum)
```

```python
from functools import partial

import jax
import jax.numpy as jnp
from jax import lax
from jax.experimental import pallas as pl
from jax.experimental.pallas import tpu as pltpu
from jax.sharding import PartitionSpec as P

beta_rate = 0.9
peak_rate = 0.1
warm_steps = 64.0
MESH = pl.DeviceIdType.MESH
F32 = jnp.float32
BF16 = jnp.bfloat16
PLANE = 4


def step_kernel(bit, dims, x_ref, c_ref, w_ref, m_ref, step_ref,
                act_ref, dg_ref, nw_ref, nm_ref,
                xc, gc, xt, wg, w32, wf, wb, g32, gb, pr, keep, sb, r1, s2, r2, tot, ptot,
                pw, pm, acc_a, acc_d,
                g_send, g_recv, e_send, e_recv, p_send, p_recv, a_send, a_recv,
                b_send, b_recv, t_send, t_recv, out_sem):
    S, R, RP, C, images, HH, WW = dims
    H = RP // 2
    LN = S // PLANE
    KR = 9 * C
    cells = HH * WW
    pad_cells = cells + 2 * WW
    CP = 384
    grp = lax.axis_index("group")
    me = lax.axis_index("shard")
    q = me // PLANE
    p = me % PLANE
    px = p + 1 - 2 * (p % 2)
    py = (p + 2) % PLANE
    pd = PLANE - 1 - p
    mask = 2 ** bit
    half = (grp // mask) % 2
    mate = grp + mask - 2 * mask * half

    def shard_at(dq, col):
        return ((q + dq) % LN) * PLANE + col

    barrier = pltpu.get_barrier_semaphore()
    peers = [(grp, shard_at(dq, p)) for dq in range(1, LN)]
    peers += [(grp, shard_at(0, col)) for col in (px, py, pd)]
    peers += [(mate, me)]
    for peer in peers:
        pl.semaphore_signal(barrier, inc=1, device_id=peer, device_id_type=MESH)

    wg[me, 0:R, :] = w_ref[...].astype(BF16)
    pl.semaphore_wait(barrier, len(peers))

    started = []

    def send(src, dst, ss, rs, peer):
        copy = pltpu.make_async_remote_copy(src_ref=src, dst_ref=dst, send_sem=ss, recv_sem=rs,
                                            device_id=peer, device_id_type=MESH)
        copy.start()
        started.append(copy)

    def arrived(ref, sem):
        pltpu.make_async_copy(ref, ref, sem).wait()

    g_count = [0]

    def send_piece(slot, peer):
        send(wg.at[slot], wg.at[slot], g_send.at[g_count[0]], g_recv.at[slot], peer)
        g_count[0] += 1

    def wait_piece(slot):
        arrived(wg.at[slot], g_recv.at[slot])

    for dq in range(1, LN):
        send_piece(me, (grp, shard_at(dq, p)))
    x_peer = (grp, shard_at(0, px))
    y_peer = (grp, shard_at(0, py))
    send_piece(me, x_peer)
    send_piece(me, y_peer)
    send(w_ref, pw, e_send.at[0], e_recv.at[0], (mate, me))
    send(m_ref, pm, e_send.at[1], e_recv.at[1], (mate, me))

    def pass_line(dq):
        slot = shard_at(dq, p)
        wait_piece(slot)
        send_piece(slot, x_peer)
        send_piece(slot, y_peer)

    def pass_plane(dq):
        slot_x = shard_at(dq, px)
        slot_y = shard_at(dq, py)
        wait_piece(slot_x)
        wait_piece(slot_y)
        if dq % 2 == 0:
            send_piece(slot_x, y_peer)
        else:
            send_piece(slot_y, x_peer)

    CH = 8 * WW
    for buf in (xc, gc):
        for img in range(images):
            buf[img, 0:WW, :] = jnp.zeros((WW, 3 * CP), BF16)
            buf[img, WW + cells:, :] = jnp.zeros((WW, 3 * CP), BF16)

    def shifted(src, buf, sign):
        def body(k, _):
            img = k // (cells // CH)
            row = (k % (cells // CH)) * CH
            mid = src[pl.ds(pl.multiple_of(k * CH, CH), CH), :]
            val = jnp.concatenate([mid.astype(F32), jnp.zeros((CH, CP - C), F32)], 1)
            col = lax.broadcasted_iota(jnp.int32, (CH, CP), 0) % WW
            prev = jnp.where(col == 0, 0.0, pltpu.roll(val, 1, 0)).astype(BF16)
            nxt = jnp.where(col == WW - 1, 0.0, pltpu.roll(val, CH - 1, 0)).astype(BF16)
            first, last = (prev, nxt) if sign > 0 else (nxt, prev)
            dst = pl.ds(pl.multiple_of(WW + row, WW), CH)
            buf[img, dst, 0:CP] = first
            buf[img, dst, CP:2 * CP] = val.astype(BF16)
            buf[img, dst, 2 * CP:3 * CP] = last
            return 0
        lax.fori_loop(0, images * (cells // CH), body, 0)

    shifted(c_ref, gc, -1)
    for img in range(images):
        xt[img] = x_ref[img * cells:(img + 1) * cells, :].T

    def tap_rows(a):
        total = None
        for img in range(images):
            part = jnp.dot(xt[img], gc[img, WW - WW * (a - 1):WW - WW * (a - 1) + cells, :],
                           preferred_element_type=F32)
            total = part if total is None else total + part
        for b in range(3):
            t = 3 * a + b
            g32[t * C:(t + 1) * C, :] = total[:, b * CP:b * CP + C]

    def send_half(u):
        for s in range(u * PLANE, (u + 1) * PLANE):
            gb[s, 0:R, :] = g32[s * R:(s + 1) * R, :]
            gb[s, R:RP, :] = jnp.zeros((RP - R, C), F32)
        src = gb.at[pl.ds(u * PLANE, PLANE), pl.ds(pl.multiple_of((1 - half) * H, 16), H), :]
        send(src, pr.at[pl.ds(u * PLANE, PLANE)], p_send.at[u], p_recv.at[u], (mate, me))

    done = 0
    lines = list(range(1, LN))
    for a in range(3):
        tap_rows(a)
        while done < LN and (done + 1) * PLANE * R <= (a + 1) * 3 * C:
            send_half(done)
            done += 1
        for dq in lines[a * len(lines) // 3:(a + 1) * len(lines) // 3]:
            pass_line(dq)

    shifted(x_ref, xc, 1)

    for u in range(LN):
        arrived(pr.at[pl.ds(u * PLANE, PLANE)], p_recv.at[u])
    mine = pl.ds(pl.multiple_of(half * H, 16), H)
    cols = [(px, 0), (py, 1), (pd, 2)]
    for dq in list(range(1, LN)) + [0]:
        for col, k in cols:
            s = shard_at(dq, col)
            sb[k, dq] = (gb[s, mine, :] + pr[s]).astype(BF16)
            send(sb.at[k, dq], r1.at[k, dq], a_send.at[k, dq], a_recv.at[k, dq], (grp, shard_at(0, col)))

    for dq in range(LN):
        pass_plane(dq)
    for dq in range(LN):
        wait_piece(shard_at(dq, pd))

    for s in range(S):
        w32[s * R:(s + 1) * R, :] = wg[s].astype(F32)[0:R]
    for t in range(9):
        a, b = t // 3, t % 3
        tap = w32[t * C:(t + 1) * C, :]
        wf[a, b * CP:b * CP + C, :] = tap.astype(BF16)
        wb[a, b * CP:b * CP + C, :] = tap.T.astype(BF16)
        for dst in (wf, wb):
            dst[a, b * CP + C:(b + 1) * CP, :] = jnp.zeros((CP - C, C), BF16)

    outs = []
    MT = cells // 2

    def conv(buf, ker, acc, out, sign, sem):
        for img in range(images):
            for part in range(cells // MT):
                row = part * MT
                val = None
                for a in range(3):
                    lo = WW + sign * WW * (a - 1) + row
                    term = jnp.dot(buf[img, lo:lo + MT, :], ker[a], preferred_element_type=F32)
                    val = term if val is None else val + term
                at = img * cells + row
                acc[at:at + MT, :] = val
                copy = pltpu.make_async_copy(acc.at[pl.ds(at, MT)], out.at[pl.ds(at, MT)],
                                             out_sem.at[sem, img * (cells // MT) + part])
                copy.start()
                outs.append(copy)

    conv(xc, wf, acc_a, act_ref, 1, 0)

    def plane_sum(dq):
        s = shard_at(dq, p)
        total = gb[s, mine, :] + pr[s]
        for k in range(3):
            arrived(r1.at[k, dq], a_recv.at[k, dq])
            total = total + r1[k, dq].astype(F32)
        return total

    for dq in range(1, LN):
        s2[dq - 1] = plane_sum(dq).astype(BF16)
        send(s2.at[dq - 1], r2.at[dq - 1], b_send.at[dq - 1], b_recv.at[dq - 1], (grp, shard_at(dq, p)))
    keep[...] = plane_sum(0)

    conv(gc, wb, acc_d, dg_ref, -1, 1)

    total = keep[...]
    for k in range(LN - 1):
        arrived(r2.at[k], b_recv.at[k])
        total = total + r2[k].astype(F32)
    tot[mine, :] = total
    send(tot.at[mine], tot.at[mine], t_send, t_recv, (mate, me))
    arrived(pw, e_recv.at[0])
    arrived(pm, e_recv.at[1])
    other = pl.ds(pl.multiple_of((1 - half) * H, 16), H)
    arrived(tot.at[other], t_recv)
    cells_group = S * images * cells
    grad = tot[0:R, :] * (0.5 * float(cells_group) ** -0.5)
    rate = peak_rate * (step_ref[0] + 1).astype(F32) / warm_steps
    moment = 0.5 * beta_rate * (m_ref[...] + pm[...]) + grad
    nm_ref[...] = moment
    nw_ref[...] = 0.5 * (w_ref[...] + pw[...]) - rate * moment

    for copy in started:
        copy.wait_send()
    for copy in outs:
        copy.wait()


def run_step(latents, cotangent, weights, momentum, step, bit):
    S = lax.axis_size("shard")
    images, HH, WW, C = latents.shape
    R = weights.shape[1]
    RP = -(-R // 32) * 32
    H = RP // 2
    LN = S // PLANE
    cells = HH * WW
    CP = 384
    dims = (S, R, RP, C, images, HH, WW)
    vmem = pl.BlockSpec(memory_space=pltpu.VMEM)
    smem = pl.BlockSpec(memory_space=pltpu.SMEM)
    hbm = pl.BlockSpec(memory_space=pl.ANY)
    V = pltpu.VMEM
    dma = pltpu.SemaphoreType.DMA
    flat = images * cells
    scratch = [
        V((images, cells + 2 * WW, 3 * CP), BF16),
        V((images, cells + 2 * WW, 3 * CP), BF16),
        V((images, C, cells), BF16),
        V((S, RP, C), BF16),
        V((9 * C, C), F32),
        V((3, 3 * CP, C), BF16),
        V((3, 3 * CP, C), BF16),
        V((9 * C, C), F32),
        V((S, RP, C), F32),
        V((S, H, C), F32),
        V((H, C), F32),
        V((3, LN, H, C), BF16),
        V((3, LN, H, C), BF16),
        V((LN - 1, H, C), BF16),
        V((LN - 1, H, C), BF16),
        V((RP, C), F32),
        V((8, 128), F32),
        V((R, C), F32),
        V((R, C), F32),
        V((flat, C), F32),
        V((flat, C), F32),
        dma((4 * LN + 1,)), dma((S,)),
        dma((2,)), dma((2,)),
        dma((LN,)), dma((LN,)),
        dma((3, LN)), dma((3, LN)),
        dma((LN - 1,)), dma((LN - 1,)),
        dma, dma,
        dma((2, 2 * images)),
    ]
    flops = 6 * flat * 9 * C * C
    act, dg, nw, nm = pl.pallas_call(
        partial(step_kernel, bit, dims),
        out_shape=(
            jax.ShapeDtypeStruct((flat, C), F32),
            jax.ShapeDtypeStruct((flat, C), F32),
            jax.ShapeDtypeStruct((R, C), F32),
            jax.ShapeDtypeStruct((R, C), F32),
        ),
        in_specs=[vmem, vmem, vmem, vmem, smem],
        out_specs=(hbm, hbm, vmem, vmem),
        scratch_shapes=scratch,
        compiler_params=pltpu.CompilerParams(
            collective_id=bit, has_side_effects=True, vmem_limit_bytes=60 * 1024 * 1024),
        cost_estimate=pl.CostEstimate(flops=flops, bytes_accessed=12 * flat * C, transcendentals=0),
    )(latents.reshape(flat, C), cotangent.reshape(flat, C), weights[0], momentum[0], step)
    return act.reshape(latents.shape), dg.reshape(latents.shape), nw[None], nm[None]


def shards(latents, cotangent, weights, momentum, step):
    bit_count = lax.axis_size("group").bit_length() - 1
    branches = [partial(run_step, bit=bit) for bit in range(bit_count)]
    args = (latents, cotangent, weights, momentum, step)
    if bit_count == 1:
        return branches[0](*args)
    return lax.switch(step[0] % bit_count, branches, *args)


def solution(mesh):
    placed = (
        P(("group", "shard"), None, None, None),
        P(("group", "shard"), None, None, None),
        P("group", "shard", None),
        P("group", "shard", None),
        P(),
    )
    return jax.shard_map(
        shards,
        mesh=mesh,
        in_specs=placed,
        out_specs=(
            P(("group", "shard"), None, None, None),
            P(("group", "shard"), None, None, None),
            P("group", "shard", None),
            P("group", "shard", None),
        ),
        check_vma=False,
    )
```

```python
from functools import partial

import jax
import jax.numpy as jnp
from jax import lax
from jax.experimental import pallas as pl
from jax.experimental.pallas import tpu as pltpu
from jax.sharding import PartitionSpec as P

beta_rate = 0.9
peak_rate = 0.1
warm_steps = 64.0
MESH = pl.DeviceIdType.MESH
F32 = jnp.float32
BF16 = jnp.bfloat16
PLANE = 4


def pack(rows):
    n, width = rows.shape
    full = width // 128
    parts = [rows[:, 128 * k:128 * (k + 1)] for k in range(full)]
    tail = rows[:, 128 * full:]
    return jnp.concatenate(parts + [jnp.concatenate([tail[:n // 2], tail[n // 2:]], 1)], 0)


def unpack(packed, n):
    full = (packed.shape[0] - n // 2) // n
    parts = [packed[n * k:n * (k + 1)] for k in range(full)]
    tail = packed[n * full:]
    return jnp.concatenate(parts + [jnp.concatenate([tail[:, :64], tail[:, 64:]], 0)], 1)


def step_kernel(bit, dims, x_hbm, c_hbm, w_ref, m_ref, step_ref,
                act_ref, dg_ref, nw_ref, nm_ref,
                x_ref, c_ref, xc, gc, xt, wg, w32, wf, wb, g32, gb, pr, keep, sb, r1, s2, r2, tot,
                pw, pm, wide, acc_a, acc_d,
                g_send, g_recv, e_send, e_recv, p_send, p_recv, a_send, a_recv,
                b_send, b_recv, t_send, t_recv, in_sem, out_sem):
    S, R, RP, C, images, HH, WW = dims
    H = RP // 2
    LN = S // PLANE
    cells = HH * WW
    grp = lax.axis_index("group")
    me = lax.axis_index("shard")
    q = me // PLANE
    p = me % PLANE
    px = p + 1 - 2 * (p % 2)
    py = (p + 2) % PLANE
    pd = PLANE - 1 - p
    mask = 2 ** bit
    half = (grp // mask) % 2
    mate = grp + mask - 2 * mask * half

    def shard_at(dq, col):
        return ((q + dq) % LN) * PLANE + col

    barrier = pltpu.get_barrier_semaphore()
    peers = [(grp, shard_at(dq, p)) for dq in range(1, LN)]
    peers += [(grp, shard_at(0, col)) for col in (px, py, pd)]
    peers += [(mate, me)]
    for peer in peers:
        pl.semaphore_signal(barrier, inc=1, device_id=peer, device_id_type=MESH)

    in_x = pltpu.make_async_copy(x_hbm, x_ref, in_sem.at[0])
    in_c = pltpu.make_async_copy(c_hbm, c_ref, in_sem.at[1])
    in_c.start()
    in_x.start()
    own = w_ref[:, 0, :]
    wg[me, 0] = pack(own[0:H]).astype(BF16)
    wg[me, 1] = pack(jnp.concatenate([own[H:R], jnp.zeros((RP - R, C), F32)], 0)).astype(BF16)
    pl.semaphore_wait(barrier, len(peers))

    started = []

    def send(src, dst, ss, rs, peer):
        copy = pltpu.make_async_remote_copy(src_ref=src, dst_ref=dst, send_sem=ss, recv_sem=rs,
                                            device_id=peer, device_id_type=MESH)
        copy.start()
        started.append(copy)

    def arrived(ref, sem):
        pltpu.make_async_copy(ref, ref, sem).wait()

    g_count = [0]

    def send_piece(slot, peer):
        send(wg.at[slot], wg.at[slot], g_send.at[g_count[0]], g_recv.at[slot], peer)
        g_count[0] += 1

    def wait_piece(slot):
        arrived(wg.at[slot], g_recv.at[slot])

    for dq in range(1, LN):
        send_piece(me, (grp, shard_at(dq, p)))
    x_peer = (grp, shard_at(0, px))
    y_peer = (grp, shard_at(0, py))
    send_piece(me, x_peer)
    send_piece(me, y_peer)
    send(w_ref, pw, e_send.at[0], e_recv.at[0], (mate, me))
    send(m_ref, pm, e_send.at[1], e_recv.at[1], (mate, me))

    def pass_line(dq):
        slot = shard_at(dq, p)
        wait_piece(slot)
        send_piece(slot, x_peer)
        send_piece(slot, y_peer)

    def pass_plane(dq):
        slot_x = shard_at(dq, px)
        slot_y = shard_at(dq, py)
        wait_piece(slot_x)
        wait_piece(slot_y)
        if dq % 2 == 0:
            send_piece(slot_x, y_peer)
        else:
            send_piece(slot_y, x_peer)

    CH = 8 * WW
    for buf in (xc, gc):
        for img in range(images):
            buf[img, 0:WW, :] = jnp.zeros((WW, 3 * C), BF16)
            buf[img, WW + cells:, :] = jnp.zeros((WW, 3 * C), BF16)

    def shifted(src, buf, sign):
        def body(k, _):
            img = k // (cells // CH)
            row = (k % (cells // CH)) * CH
            mid = src[pl.ds(pl.multiple_of(k * CH, CH), CH), :]
            val = mid.astype(F32)
            col = lax.broadcasted_iota(jnp.int32, (CH, C), 0) % WW
            prev = jnp.where(col == 0, 0.0, pltpu.roll(val, 1, 0)).astype(BF16)
            nxt = jnp.where(col == WW - 1, 0.0, pltpu.roll(val, CH - 1, 0)).astype(BF16)
            first, last = (prev, nxt) if sign > 0 else (nxt, prev)
            dst = pl.ds(pl.multiple_of(WW + row, WW), CH)
            buf[img, dst, :] = jnp.concatenate([first, mid, last], 1)
            return 0
        lax.fori_loop(0, images * (cells // CH), body, 0)

    in_c.wait()
    shifted(c_ref, gc, -1)
    in_x.wait()
    for img in range(images):
        xt[img] = x_ref[img * cells:(img + 1) * cells, :].T
    pass_plane(0)

    def tap_rows(a):
        total = None
        for img in range(images):
            part = jnp.dot(xt[img], gc[img, WW - WW * (a - 1):WW - WW * (a - 1) + cells, :],
                           preferred_element_type=F32)
            total = part if total is None else total + part
        for b in range(3):
            t = 3 * a + b
            g32[t * C:(t + 1) * C, :] = total[:, b * C:(b + 1) * C]

    def send_half(u):
        for s in range(u * PLANE, (u + 1) * PLANE):
            gb[s, 0] = pack(g32[s * R:s * R + H, :])
            gb[s, 1] = pack(jnp.concatenate([g32[s * R + H:(s + 1) * R, :], jnp.zeros((RP - R, C), F32)], 0))
        group = pl.ds(u * PLANE, PLANE)
        send(gb.at[group, 1 - half], pr.at[group], p_send.at[u], p_recv.at[u], (mate, me))

    done = 0
    lines = list(range(1, LN))
    planes = list(range(1, LN))
    for a in range(3):
        tap_rows(a)
        while done < LN and (done + 1) * PLANE * R <= (a + 1) * 3 * C:
            send_half(done)
            done += 1
        for dq in lines[a * len(lines) // 3:(a + 1) * len(lines) // 3]:
            pass_line(dq)
        for dq in planes[max(a - 1, 0) * len(planes) // 3:a * len(planes) // 3]:
            pass_plane(dq)

    shifted(x_ref, xc, 1)

    for u in range(LN):
        arrived(pr.at[pl.ds(u * PLANE, PLANE)], p_recv.at[u])
    cols = [(px, 0), (py, 1), (pd, 2)]
    for dq in list(range(1, LN)) + [0]:
        for col, k in cols:
            s = shard_at(dq, col)
            sb[k, dq] = (gb[s, half] + pr[s]).astype(BF16)
            send(sb.at[k, dq], r1.at[k, dq], a_send.at[k, dq], a_recv.at[k, dq], (grp, shard_at(0, col)))

    for dq in planes[2 * len(planes) // 3:]:
        pass_plane(dq)
    for dq in range(LN):
        wait_piece(shard_at(dq, pd))

    for s in range(S):
        w32[s * R:s * R + H, :] = unpack(wg[s, 0].astype(F32), H)
        w32[s * R + H:(s + 1) * R, :] = unpack(wg[s, 1].astype(F32), H)[0:R - H]
    for a in range(3):
        wf[:, a * C:(a + 1) * C] = w32[3 * a * C:3 * (a + 1) * C, :].astype(BF16)
    for b in range(3):
        wb[b * C:(b + 1) * C, :] = jnp.concatenate(
            [w32[(3 * a + b) * C:(3 * a + b + 1) * C, :].astype(BF16).T for a in range(3)], 1)

    outs = []

    def conv(buf, ker, acc, out, sign, sem):
        for img in range(images):
            wide[...] = jnp.dot(buf[img], ker[...], preferred_element_type=F32)
            val = None
            for a in range(3):
                lo = WW + sign * WW * (a - 1)
                term = wide[lo:lo + cells, a * C:(a + 1) * C]
                val = term if val is None else val + term
            rows = pl.ds(img * cells, cells)
            acc[rows, :] = val
            copy = pltpu.make_async_copy(acc.at[rows], out.at[rows], out_sem.at[sem, img])
            copy.start()
            outs.append(copy)

    conv(xc, wf, acc_a, act_ref, 1, 0)

    def plane_sum(dq):
        s = shard_at(dq, p)
        total = gb[s, half] + pr[s]
        for k in range(3):
            arrived(r1.at[k, dq], a_recv.at[k, dq])
            total = total + r1[k, dq].astype(F32)
        return total

    for dq in range(1, LN):
        s2[dq - 1] = plane_sum(dq).astype(BF16)
        send(s2.at[dq - 1], r2.at[dq - 1], b_send.at[dq - 1], b_recv.at[dq - 1], (grp, shard_at(dq, p)))
    keep[...] = plane_sum(0)

    conv(gc, wb, acc_d, dg_ref, -1, 1)

    total = keep[...]
    for k in range(LN - 1):
        arrived(r2.at[k], b_recv.at[k])
        total = total + r2[k].astype(F32)
    tot[half] = total
    send(tot.at[half], tot.at[half], t_send, t_recv, (mate, me))
    arrived(pw, e_recv.at[0])
    arrived(pm, e_recv.at[1])
    arrived(tot.at[1 - half], t_recv)
    cells_group = S * images * cells
    rows = jnp.concatenate([unpack(tot[0], H), unpack(tot[1], H)[0:R - H]], 0)
    grad = rows * (0.5 * float(cells_group) ** -0.5)
    rate = peak_rate * (step_ref[0] + 1).astype(F32) / warm_steps
    moment = 0.5 * beta_rate * (m_ref[:, 0, :] + pm[:, 0, :]) + grad
    nm_ref[:, 0, :] = moment
    nw_ref[:, 0, :] = 0.5 * (w_ref[:, 0, :] + pw[:, 0, :]) - rate * moment

    for copy in started:
        copy.wait_send()
    for copy in outs:
        copy.wait()


def run_step(latents, cotangent, weights, momentum, step, bit):
    S = lax.axis_size("shard")
    images, HH, WW, C = latents.shape
    R = weights.shape[1]
    RP = -(-R // 64) * 64
    H = RP // 2
    LN = S // PLANE
    cells = HH * WW
    PK = H * C // 128
    dims = (S, R, RP, C, images, HH, WW)
    vmem = pl.BlockSpec(memory_space=pltpu.VMEM)
    smem = pl.BlockSpec(memory_space=pltpu.SMEM)
    hbm = pl.BlockSpec(memory_space=pl.ANY)
    V = pltpu.VMEM
    dma = pltpu.SemaphoreType.DMA
    flat = images * cells
    scratch = [
        V((flat, C), BF16),
        V((flat, C), BF16),
        V((images, cells + 2 * WW, 3 * C), BF16),
        V((images, cells + 2 * WW, 3 * C), BF16),
        V((images, C, cells), BF16),
        V((S, 2, PK, 128), BF16),
        V((9 * C, C), F32),
        V((3 * C, 3 * C), BF16),
        V((3 * C, 3 * C), BF16),
        V((9 * C, C), F32),
        V((S, 2, PK, 128), F32),
        V((S, PK, 128), F32),
        V((PK, 128), F32),
        V((3, LN, PK, 128), BF16),
        V((3, LN, PK, 128), BF16),
        V((LN - 1, PK, 128), BF16),
        V((LN - 1, PK, 128), BF16),
        V((2, PK, 128), F32),
        V((R, 1, C), F32),
        V((R, 1, C), F32),
        V((cells + 2 * WW, 3 * C), F32),
        V((flat, C), F32),
        V((flat, C), F32),
        dma((4 * LN + 1,)), dma((S,)),
        dma((2,)), dma((2,)),
        dma((LN,)), dma((LN,)),
        dma((3, LN)), dma((3, LN)),
        dma((LN - 1,)), dma((LN - 1,)),
        dma, dma,
        dma((2,)),
        dma((2, images)),
    ]
    flops = 6 * flat * 9 * C * C
    act, dg, nw, nm = pl.pallas_call(
        partial(step_kernel, bit, dims),
        out_shape=(
            jax.ShapeDtypeStruct((flat, C), F32),
            jax.ShapeDtypeStruct((flat, C), F32),
            jax.ShapeDtypeStruct((R, 1, C), F32),
            jax.ShapeDtypeStruct((R, 1, C), F32),
        ),
        in_specs=[hbm, hbm, vmem, vmem, smem],
        out_specs=(hbm, hbm, vmem, vmem),
        scratch_shapes=scratch,
        compiler_params=pltpu.CompilerParams(
            collective_id=bit, has_side_effects=True, vmem_limit_bytes=60 * 1024 * 1024),
        cost_estimate=pl.CostEstimate(flops=flops, bytes_accessed=12 * flat * C, transcendentals=0),
    )(latents.reshape(flat, C), cotangent.reshape(flat, C), weights.transpose(1, 0, 2), momentum.transpose(1, 0, 2), step)
    return act.reshape(latents.shape), dg.reshape(latents.shape), nw.transpose(1, 0, 2), nm.transpose(1, 0, 2)


def shards(latents, cotangent, weights, momentum, step):
    bit_count = lax.axis_size("group").bit_length() - 1
    branches = [partial(run_step, bit=bit) for bit in range(bit_count)]
    args = (latents, cotangent, weights, momentum, step)
    if bit_count == 1:
        return branches[0](*args)
    return lax.switch(step[0] % bit_count, branches, *args)


def solution(mesh):
    placed = (
        P(("group", "shard"), None, None, None),
        P(("group", "shard"), None, None, None),
        P("group", "shard", None),
        P("group", "shard", None),
        P(),
    )
    return jax.shard_map(
        shards,
        mesh=mesh,
        in_specs=placed,
        out_specs=(
            P(("group", "shard"), None, None, None),
            P(("group", "shard"), None, None, None),
            P("group", "shard", None),
            P("group", "shard", None),
        ),
        check_vma=False,
    )
```

```python
from functools import partial

import jax
import jax.numpy as jnp
from jax import lax
from jax.experimental import pallas as pl
from jax.experimental.pallas import tpu as pltpu
from jax.sharding import PartitionSpec as P

beta_rate = 0.9
peak_rate = 0.1
warm_steps = 64.0
MESH = pl.DeviceIdType.MESH
F32 = jnp.float32
BF16 = jnp.bfloat16
PLANE = 4


def pack(rows):
    n, width = rows.shape
    full = width // 128
    parts = [rows[:, 128 * k:128 * (k + 1)] for k in range(full)]
    tail = rows[:, 128 * full:]
    return jnp.concatenate(parts + [jnp.concatenate([tail[:n // 2], tail[n // 2:]], 1)], 0)


def unpack(packed, n):
    full = (packed.shape[0] - n // 2) // n
    parts = [packed[n * k:n * (k + 1)] for k in range(full)]
    tail = packed[n * full:]
    return jnp.concatenate(parts + [jnp.concatenate([tail[:, :64], tail[:, 64:]], 0)], 1)


def step_kernel(bit, dims, x_hbm, c_hbm, w_ref, m_ref, step_ref,
                act_ref, dg_ref, nw_ref, nm_ref,
                x_ref, c_ref, xc, gc, xt, wg, wf, wb, g32, gb, pr, keep, sb, r1, s2, r2, tot,
                pw, pm, wide, acc,
                g_send, g_recv, e_send, e_recv, p_send, p_recv, a_send, a_recv,
                b_send, b_recv, t_send, t_recv, in_sem, out_sem):
    S, R, RP, C, images, HH, WW = dims
    H = RP // 2
    LN = S // PLANE
    cells = HH * WW
    grp = lax.axis_index("group")
    me = lax.axis_index("shard")
    q = me // PLANE
    p = me % PLANE
    px = p + 1 - 2 * (p % 2)
    py = (p + 2) % PLANE
    pd = PLANE - 1 - p
    mask = 2 ** bit
    half = (grp // mask) % 2
    mate = grp + mask - 2 * mask * half

    def shard_at(dq, col):
        return ((q + dq) % LN) * PLANE + col

    barrier = pltpu.get_barrier_semaphore()
    peers = [(grp, shard_at(dq, p)) for dq in range(1, LN)]
    peers += [(grp, shard_at(0, col)) for col in (px, py, pd)]
    peers += [(mate, me)]
    for peer in peers:
        pl.semaphore_signal(barrier, inc=1, device_id=peer, device_id_type=MESH)

    in_x = pltpu.make_async_copy(x_hbm, x_ref, in_sem.at[0])
    in_c = pltpu.make_async_copy(c_hbm, c_ref, in_sem.at[1])
    in_c.start()
    in_x.start()
    own = w_ref[:, 0, :]
    wg[me, 0] = pack(own[0:H]).astype(BF16)
    wg[me, 1] = pack(jnp.concatenate([own[H:R], jnp.zeros((RP - R, C), F32)], 0)).astype(BF16)
    pl.semaphore_wait(barrier, len(peers))

    started = []

    def send(src, dst, ss, rs, peer):
        copy = pltpu.make_async_remote_copy(src_ref=src, dst_ref=dst, send_sem=ss, recv_sem=rs,
                                            device_id=peer, device_id_type=MESH)
        copy.start()
        started.append(copy)

    def arrived(ref, sem):
        pltpu.make_async_copy(ref, ref, sem).wait()

    g_count = [0]

    def send_piece(slot, peer):
        send(wg.at[slot], wg.at[slot], g_send.at[g_count[0]], g_recv.at[slot], peer)
        g_count[0] += 1

    def wait_piece(slot):
        arrived(wg.at[slot], g_recv.at[slot])

    for dq in range(1, LN):
        send_piece(me, (grp, shard_at(dq, p)))
    x_peer = (grp, shard_at(0, px))
    y_peer = (grp, shard_at(0, py))
    send_piece(me, x_peer)
    send_piece(me, y_peer)
    send(w_ref, pw, e_send.at[0], e_recv.at[0], (mate, me))
    send(m_ref, pm, e_send.at[1], e_recv.at[1], (mate, me))

    def pass_line(dq):
        slot = shard_at(dq, p)
        wait_piece(slot)
        send_piece(slot, x_peer)
        send_piece(slot, y_peer)

    def pass_plane(dq):
        slot_x = shard_at(dq, px)
        slot_y = shard_at(dq, py)
        wait_piece(slot_x)
        wait_piece(slot_y)
        if dq % 2 == 0:
            send_piece(slot_x, y_peer)
        else:
            send_piece(slot_y, x_peer)

    CH = 8 * WW
    for buf in (xc, gc):
        for img in range(images):
            buf[img, 0:WW, :] = jnp.zeros((WW, 3 * C), BF16)
            buf[img, WW + cells:, :] = jnp.zeros((WW, 3 * C), BF16)

    def shifted(src, buf, sign):
        def body(k, _):
            img = k // (cells // CH)
            row = (k % (cells // CH)) * CH
            mid = src[pl.ds(pl.multiple_of(k * CH, CH), CH), :]
            val = mid.astype(F32)
            col = lax.broadcasted_iota(jnp.int32, (CH, C), 0) % WW
            prev = jnp.where(col == 0, 0.0, pltpu.roll(val, 1, 0)).astype(BF16)
            nxt = jnp.where(col == WW - 1, 0.0, pltpu.roll(val, CH - 1, 0)).astype(BF16)
            first, last = (prev, nxt) if sign > 0 else (nxt, prev)
            dst = pl.ds(pl.multiple_of(WW + row, WW), CH)
            buf[img, dst, :] = jnp.concatenate([first, mid, last], 1)
            return 0
        lax.fori_loop(0, images * (cells // CH), body, 0)

    in_c.wait()
    shifted(c_ref, gc, -1)
    in_x.wait()
    for img in range(images):
        xt[img] = x_ref[img * cells:(img + 1) * cells, :].T

    order = []
    for dq in range(1, LN // 2 + 1):
        order += [dq, LN - dq] if 2 * dq != LN else [dq]
    tasks = [partial(pass_line, order[0]), partial(pass_plane, 0)]
    tasks += [partial(pass_line, dq) for dq in order[1:]]
    tasks += [partial(pass_plane, dq) for dq in order]
    points = 3 * images + 1
    turn = [0]

    def pass_on():
        lo, hi = turn[0] * len(tasks) // points, (turn[0] + 1) * len(tasks) // points
        for task in tasks[lo:hi]:
            task()
        turn[0] += 1

    pass_on()

    def tap_rows(a):
        total = None
        for img in range(images):
            part = jnp.dot(xt[img], gc[img, WW - WW * (a - 1):WW - WW * (a - 1) + cells, :],
                           preferred_element_type=F32)
            total = part if total is None else total + part
            pass_on()
        for b in range(3):
            t = 3 * a + b
            g32[t * C:(t + 1) * C, :] = total[:, b * C:(b + 1) * C]

    def send_half(u):
        for s in range(u * PLANE, (u + 1) * PLANE):
            gb[s, 0] = pack(g32[s * R:s * R + H, :])
            gb[s, 1] = pack(jnp.concatenate([g32[s * R + H:(s + 1) * R, :], jnp.zeros((RP - R, C), F32)], 0))
        group = pl.ds(u * PLANE, PLANE)
        send(gb.at[group, 1 - half], pr.at[group], p_send.at[u], p_recv.at[u], (mate, me))

    cols = [(px, 0), (py, 1), (pd, 2)]

    def send_plane(u):
        arrived(pr.at[pl.ds(u * PLANE, PLANE)], p_recv.at[u])
        for col, k in cols:
            sb[k, u] = (gb[u * PLANE + col, half] + pr[u * PLANE + col]).astype(BF16)
            send(sb.at[k, u], r1.at[k, u], a_send.at[k, u], a_recv.at[k, u], (grp, shard_at(0, col)))

    done = 0
    sent = 0
    for a in range(3):
        tap_rows(a)
        ready = done
        while done < LN and (done + 1) * PLANE * R <= (a + 1) * 3 * C:
            send_half(done)
            done += 1
        while sent < ready:
            send_plane(sent)
            sent += 1

    shifted(x_ref, xc, 1)
    while sent < LN:
        send_plane(sent)
        sent += 1
    for dq in range(LN):
        wait_piece(shard_at(dq, pd))

    for s in range(S):
        g32[s * R:s * R + H, :] = unpack(wg[s, 0].astype(F32), H)
        g32[s * R + H:(s + 1) * R, :] = unpack(wg[s, 1].astype(F32), H)[0:R - H]
    for a in range(3):
        wf[:, a * C:(a + 1) * C] = g32[3 * a * C:3 * (a + 1) * C, :].astype(BF16)

    outs = {}

    def conv(buf, ker, out, sign, sem, img):
        wide[...] = jnp.dot(buf[img], ker[...], preferred_element_type=F32)
        val = None
        for a in range(3):
            lo = WW + sign * WW * (a - 1)
            term = wide[lo:lo + cells, a * C:(a + 1) * C]
            val = term if val is None else val + term
        rows = pl.ds(img * cells, cells)
        if img in outs:
            outs.pop(img).wait()
        acc[rows, :] = val
        outs[img] = pltpu.make_async_copy(acc.at[rows], out.at[rows], out_sem.at[sem, img])
        outs[img].start()

    def plane_sum(dq):
        u = (q + dq) % LN
        total = gb[u * PLANE + p, half] + pr[u * PLANE + p]
        for k in range(3):
            arrived(r1.at[k, u], a_recv.at[k, u])
            total = total + r1[k, u].astype(F32)
        return total

    def send_line(dq):
        s2[dq - 1] = plane_sum(dq).astype(BF16)
        send(s2.at[dq - 1], r2.at[dq - 1], b_send.at[dq - 1], b_recv.at[dq - 1], (grp, shard_at(dq, p)))

    for img in range(images):
        conv(xc, wf, act_ref, 1, 0, img)
    for b in range(3):
        wb[b * C:(b + 1) * C, :] = jnp.concatenate(
            [g32[(3 * a + b) * C:(3 * a + b + 1) * C, :].astype(BF16).T for a in range(3)], 1)
    for dq in range(1, LN):
        send_line(dq)
    keep[...] = plane_sum(0)
    for img in range(images - 1):
        conv(gc, wb, dg_ref, -1, 1, img)

    total = keep[...]
    for k in range(LN - 1):
        arrived(r2.at[k], b_recv.at[k])
        total = total + r2[k].astype(F32)
    tot[half] = total
    send(tot.at[half], tot.at[half], t_send, t_recv, (mate, me))
    conv(gc, wb, dg_ref, -1, 1, images - 1)
    arrived(pw, e_recv.at[0])
    arrived(pm, e_recv.at[1])
    arrived(tot.at[1 - half], t_recv)
    cells_group = S * images * cells
    rows = jnp.concatenate([unpack(tot[0], H), unpack(tot[1], H)[0:R - H]], 0)
    grad = rows * (0.5 * float(cells_group) ** -0.5)
    rate = peak_rate * (step_ref[0] + 1).astype(F32) / warm_steps
    moment = 0.5 * beta_rate * (m_ref[:, 0, :] + pm[:, 0, :]) + grad
    nm_ref[:, 0, :] = moment
    nw_ref[:, 0, :] = 0.5 * (w_ref[:, 0, :] + pw[:, 0, :]) - rate * moment

    for copy in started:
        copy.wait_send()
    for copy in outs.values():
        copy.wait()


def run_step(latents, cotangent, weights, momentum, step, bit):
    S = lax.axis_size("shard")
    images, HH, WW, C = latents.shape
    R = weights.shape[1]
    RP = -(-R // 64) * 64
    H = RP // 2
    LN = S // PLANE
    cells = HH * WW
    PK = H * C // 128
    dims = (S, R, RP, C, images, HH, WW)
    vmem = pl.BlockSpec(memory_space=pltpu.VMEM)
    smem = pl.BlockSpec(memory_space=pltpu.SMEM)
    hbm = pl.BlockSpec(memory_space=pl.ANY)
    V = pltpu.VMEM
    dma = pltpu.SemaphoreType.DMA
    flat = images * cells
    scratch = [
        V((flat, C), BF16),
        V((flat, C), BF16),
        V((images, cells + 2 * WW, 3 * C), BF16),
        V((images, cells + 2 * WW, 3 * C), BF16),
        V((images, C, cells), BF16),
        V((S, 2, PK, 128), BF16),
        V((3 * C, 3 * C), BF16),
        V((3 * C, 3 * C), BF16),
        V((9 * C, C), F32),
        V((S, 2, PK, 128), F32),
        V((S, PK, 128), F32),
        V((PK, 128), F32),
        V((3, LN, PK, 128), BF16),
        V((3, LN, PK, 128), BF16),
        V((LN - 1, PK, 128), BF16),
        V((LN - 1, PK, 128), BF16),
        V((2, PK, 128), F32),
        V((R, 1, C), F32),
        V((R, 1, C), F32),
        V((cells + 2 * WW, 3 * C), F32),
        V((flat, C), F32),
        dma((4 * LN + 1,)), dma((S,)),
        dma((2,)), dma((2,)),
        dma((LN,)), dma((LN,)),
        dma((3, LN)), dma((3, LN)),
        dma((LN - 1,)), dma((LN - 1,)),
        dma, dma,
        dma((2,)),
        dma((2, images)),
    ]
    flops = 6 * flat * 9 * C * C
    act, dg, nw, nm = pl.pallas_call(
        partial(step_kernel, bit, dims),
        out_shape=(
            jax.ShapeDtypeStruct((flat, C), F32),
            jax.ShapeDtypeStruct((flat, C), F32),
            jax.ShapeDtypeStruct((R, 1, C), F32),
            jax.ShapeDtypeStruct((R, 1, C), F32),
        ),
        in_specs=[hbm, hbm, vmem, vmem, smem],
        out_specs=(hbm, hbm, vmem, vmem),
        scratch_shapes=scratch,
        compiler_params=pltpu.CompilerParams(
            collective_id=bit, has_side_effects=True, vmem_limit_bytes=60 * 1024 * 1024),
        cost_estimate=pl.CostEstimate(flops=flops, bytes_accessed=12 * flat * C, transcendentals=0),
    )(latents.reshape(flat, C), cotangent.reshape(flat, C), weights.transpose(1, 0, 2), momentum.transpose(1, 0, 2), step)
    return act.reshape(latents.shape), dg.reshape(latents.shape), nw.transpose(1, 0, 2), nm.transpose(1, 0, 2)


def shards(latents, cotangent, weights, momentum, step):
    bit_count = lax.axis_size("group").bit_length() - 1
    branches = [partial(run_step, bit=bit) for bit in range(bit_count)]
    args = (latents, cotangent, weights, momentum, step)
    if bit_count == 1:
        return branches[0](*args)
    return lax.switch(step[0] % bit_count, branches, *args)


def solution(mesh):
    placed = (
        P(("group", "shard"), None, None, None),
        P(("group", "shard"), None, None, None),
        P("group", "shard", None),
        P("group", "shard", None),
        P(),
    )
    return jax.shard_map(
        shards,
        mesh=mesh,
        in_specs=placed,
        out_specs=(
            P(("group", "shard"), None, None, None),
            P(("group", "shard"), None, None, None),
            P("group", "shard", None),
            P("group", "shard", None),
        ),
        check_vma=False,
    )
```

```python
from functools import partial

import jax
import jax.numpy as jnp
from jax import lax
from jax.experimental import pallas as pl
from jax.experimental.pallas import tpu as pltpu
from jax.sharding import PartitionSpec as P

beta_rate = 0.9
peak_rate = 0.1
warm_steps = 64.0
MESH = pl.DeviceIdType.MESH
F32 = jnp.float32
BF16 = jnp.bfloat16
PLANE = 4


def pack(rows):
    n, width = rows.shape
    full = width // 128
    parts = [rows[:, 128 * k:128 * (k + 1)] for k in range(full)]
    tail = rows[:, 128 * full:]
    return jnp.concatenate(parts + [jnp.concatenate([tail[:n // 2], tail[n // 2:]], 1)], 0)


def unpack(packed, n):
    full = (packed.shape[0] - n // 2) // n
    parts = [packed[n * k:n * (k + 1)] for k in range(full)]
    tail = packed[n * full:]
    return jnp.concatenate(parts + [jnp.concatenate([tail[:, :64], tail[:, 64:]], 0)], 1)


def step_kernel(bit, dims, x_hbm, c_hbm, w_ref, m_ref, step_ref,
                act_ref, dg_ref, nw_ref, nm_ref,
                x_ref, c_ref, xc, gc, xt, wg, wf, wb, g32, gb, pr, keep, sb, r1, s2, r2, tot,
                pw, pm, wide, acc,
                g_send, g_recv, e_send, e_recv, p_send, p_recv, a_send, a_recv,
                b_send, b_recv, t_send, t_recv, in_sem, out_sem):
    S, R, RP, C, images, HH, WW = dims
    H = RP // 2
    LN = S // PLANE
    cells = HH * WW
    grp = lax.axis_index("group")
    me = lax.axis_index("shard")
    q = me // PLANE
    p = me % PLANE
    px = p + 1 - 2 * (p % 2)
    py = (p + 2) % PLANE
    pd = PLANE - 1 - p
    mask = 2 ** bit
    half = (grp // mask) % 2
    mate = grp + mask - 2 * mask * half

    def shard_at(dq, col):
        return ((q + dq) % LN) * PLANE + col

    barrier = pltpu.get_barrier_semaphore()
    peers = [(grp, shard_at(dq, p)) for dq in range(1, LN)]
    peers += [(grp, shard_at(0, col)) for col in (px, py, pd)]
    peers += [(mate, me)]
    for peer in peers:
        pl.semaphore_signal(barrier, inc=1, device_id=peer, device_id_type=MESH)

    in_x = pltpu.make_async_copy(x_hbm, x_ref, in_sem.at[0])
    in_c = pltpu.make_async_copy(c_hbm, c_ref, in_sem.at[1])
    in_c.start()
    in_x.start()
    own = w_ref[:, 0, :]
    wg[me, 0] = pack(own[0:H]).astype(BF16)
    wg[me, 1] = pack(jnp.concatenate([own[H:R], jnp.zeros((RP - R, C), F32)], 0)).astype(BF16)
    pl.semaphore_wait(barrier, len(peers))

    started = []

    def send(src, dst, ss, rs, peer):
        copy = pltpu.make_async_remote_copy(src_ref=src, dst_ref=dst, send_sem=ss, recv_sem=rs,
                                            device_id=peer, device_id_type=MESH)
        copy.start()
        started.append(copy)

    def arrived(ref, sem):
        pltpu.make_async_copy(ref, ref, sem).wait()

    g_count = [0]

    def send_piece(slot, peer):
        send(wg.at[slot], wg.at[slot], g_send.at[g_count[0]], g_recv.at[slot], peer)
        g_count[0] += 1

    def wait_piece(slot):
        arrived(wg.at[slot], g_recv.at[slot])

    for dq in range(1, LN):
        send_piece(me, (grp, shard_at(dq, p)))
    x_peer = (grp, shard_at(0, px))
    y_peer = (grp, shard_at(0, py))
    send_piece(me, x_peer)
    send_piece(me, y_peer)
    send(w_ref, pw, e_send.at[0], e_recv.at[0], (mate, me))
    send(m_ref, pm, e_send.at[1], e_recv.at[1], (mate, me))

    def pass_line(dq):
        slot = shard_at(dq, p)
        wait_piece(slot)
        send_piece(slot, x_peer)
        send_piece(slot, y_peer)

    def pass_plane(dq):
        slot_x = shard_at(dq, px)
        slot_y = shard_at(dq, py)
        wait_piece(slot_x)
        wait_piece(slot_y)
        if dq % 2 == 0:
            send_piece(slot_x, y_peer)
        else:
            send_piece(slot_y, x_peer)

    CH = 8 * WW
    for buf in (xc, gc):
        for img in range(images):
            buf[img, 0:WW, :] = jnp.zeros((WW, 3 * C), BF16)
            buf[img, WW + cells:, :] = jnp.zeros((WW, 3 * C), BF16)

    def shifted(src, buf, sign):
        def body(k, _):
            img = k // (cells // CH)
            row = (k % (cells // CH)) * CH
            mid = src[pl.ds(pl.multiple_of(k * CH, CH), CH), :]
            val = mid.astype(F32)
            col = lax.broadcasted_iota(jnp.int32, (1, WW, C), 1)
            prev = pltpu.roll(val, 1, 0).reshape(CH // WW, WW, C)
            prev = jnp.where(col == 0, 0.0, prev).reshape(CH, C).astype(BF16)
            nxt = pltpu.roll(val, CH - 1, 0).reshape(CH // WW, WW, C)
            nxt = jnp.where(col == WW - 1, 0.0, nxt).reshape(CH, C).astype(BF16)
            first, last = (prev, nxt) if sign > 0 else (nxt, prev)
            dst = pl.ds(pl.multiple_of(WW + row, WW), CH)
            buf[img, dst, :] = jnp.concatenate([first, mid, last], 1)
            return 0
        lax.fori_loop(0, images * (cells // CH), body, 0)

    in_c.wait()
    shifted(c_ref, gc, -1)
    in_x.wait()
    for img in range(images):
        xt[img] = x_ref[img * cells:(img + 1) * cells, :].T

    order = []
    for dq in range(1, LN // 2 + 1):
        order += [dq, LN - dq] if 2 * dq != LN else [dq]
    tasks = [partial(pass_line, order[0]), partial(pass_plane, 0)]
    tasks += [partial(pass_line, dq) for dq in order[1:]]
    tasks += [partial(pass_plane, dq) for dq in order]
    points = 3 * images + 1
    turn = [0]

    def pass_on():
        lo, hi = turn[0] * len(tasks) // points, (turn[0] + 1) * len(tasks) // points
        for task in tasks[lo:hi]:
            task()
        turn[0] += 1

    pass_on()

    def tap_rows(a):
        total = None
        for img in range(images):
            part = jnp.dot(xt[img], gc[img, WW - WW * (a - 1):WW - WW * (a - 1) + cells, :],
                           preferred_element_type=F32)
            total = part if total is None else total + part
            pass_on()
        for b in range(3):
            t = 3 * a + b
            g32[t * C:(t + 1) * C, :] = total[:, b * C:(b + 1) * C]

    def send_half(u):
        for s in range(u * PLANE, (u + 1) * PLANE):
            gb[s, 0] = pack(g32[s * R:s * R + H, :])
            gb[s, 1] = pack(jnp.concatenate([g32[s * R + H:(s + 1) * R, :], jnp.zeros((RP - R, C), F32)], 0))
        group = pl.ds(u * PLANE, PLANE)
        send(gb.at[group, 1 - half], pr.at[group], p_send.at[u], p_recv.at[u], (mate, me))

    cols = [(px, 0), (py, 1), (pd, 2)]

    def send_plane(u):
        arrived(pr.at[pl.ds(u * PLANE, PLANE)], p_recv.at[u])
        for col, k in cols:
            sb[k, u] = (gb[u * PLANE + col, half] + pr[u * PLANE + col]).astype(BF16)
            send(sb.at[k, u], r1.at[k, u], a_send.at[k, u], a_recv.at[k, u], (grp, shard_at(0, col)))

    done = 0
    sent = 0
    for a in range(3):
        tap_rows(a)
        ready = done
        while done < LN and (done + 1) * PLANE * R <= (a + 1) * 3 * C:
            send_half(done)
            done += 1
        while sent < ready:
            send_plane(sent)
            sent += 1

    shifted(x_ref, xc, 1)
    while sent < LN:
        send_plane(sent)
        sent += 1
    for dq in range(LN):
        wait_piece(shard_at(dq, pd))

    for s in range(S):
        g32[s * R:s * R + H, :] = unpack(wg[s, 0].astype(F32), H)
        g32[s * R + H:(s + 1) * R, :] = unpack(wg[s, 1].astype(F32), H)[0:R - H]
    for a in range(3):
        wf[:, a * C:(a + 1) * C] = g32[3 * a * C:3 * (a + 1) * C, :].astype(BF16)

    outs = {}

    def conv(buf, ker, out, sign, sem, img):
        wide[...] = jnp.dot(buf[img], ker[...], preferred_element_type=F32)
        val = None
        for a in range(3):
            lo = WW + sign * WW * (a - 1)
            term = wide[lo:lo + cells, a * C:(a + 1) * C]
            val = term if val is None else val + term
        rows = pl.ds(img * cells, cells)
        if img in outs:
            outs.pop(img).wait()
        acc[rows, :] = val
        outs[img] = pltpu.make_async_copy(acc.at[rows], out.at[rows], out_sem.at[sem, img])
        outs[img].start()

    def plane_sum(dq):
        u = (q + dq) % LN
        total = gb[u * PLANE + p, half] + pr[u * PLANE + p]
        for k in range(3):
            arrived(r1.at[k, u], a_recv.at[k, u])
            total = total + r1[k, u].astype(F32)
        return total

    def send_line(dq):
        s2[dq - 1] = plane_sum(dq).astype(BF16)
        send(s2.at[dq - 1], r2.at[dq - 1], b_send.at[dq - 1], b_recv.at[dq - 1], (grp, shard_at(dq, p)))

    for img in range(images):
        conv(xc, wf, act_ref, 1, 0, img)
    for b in range(3):
        wb[b * C:(b + 1) * C, :] = jnp.concatenate(
            [g32[(3 * a + b) * C:(3 * a + b + 1) * C, :].astype(BF16).T for a in range(3)], 1)
    for dq in range(1, LN):
        send_line(dq)
    keep[...] = plane_sum(0)
    for img in range(images - 1):
        conv(gc, wb, dg_ref, -1, 1, img)

    total = keep[...]
    for k in range(LN - 1):
        arrived(r2.at[k], b_recv.at[k])
        total = total + r2[k].astype(F32)
    tot[half] = total
    send(tot.at[half], tot.at[half], t_send, t_recv, (mate, me))
    conv(gc, wb, dg_ref, -1, 1, images - 1)
    arrived(pw, e_recv.at[0])
    arrived(pm, e_recv.at[1])
    arrived(tot.at[1 - half], t_recv)
    cells_group = S * images * cells
    rows = jnp.concatenate([unpack(tot[0], H), unpack(tot[1], H)[0:R - H]], 0)
    grad = rows * (0.5 * float(cells_group) ** -0.5)
    rate = peak_rate * (step_ref[0] + 1).astype(F32) / warm_steps
    moment = 0.5 * beta_rate * (m_ref[:, 0, :] + pm[:, 0, :]) + grad
    nm_ref[:, 0, :] = moment
    nw_ref[:, 0, :] = 0.5 * (w_ref[:, 0, :] + pw[:, 0, :]) - rate * moment

    for copy in started:
        copy.wait_send()
    for copy in outs.values():
        copy.wait()


def relay_kernel(pieces, *refs):
    count = (len(refs) - 2) // 3
    srcs, dsts, holds = refs[:count], refs[count:2 * count], refs[2 * count:3 * count]
    read_sem, write_sem = refs[3 * count:]
    spans = []
    for k in range(count):
        step = srcs[k].shape[0] // pieces[k]
        spans += [(k, pl.ds(i * step, step)) for i in range(pieces[k])]
    reads = [pltpu.make_async_copy(srcs[k].at[at], holds[k].at[at], read_sem.at[i])
             for i, (k, at) in enumerate(spans)]
    writes = [pltpu.make_async_copy(holds[k].at[at], dsts[k].at[at], write_sem.at[i])
              for i, (k, at) in enumerate(spans)]
    for copy in reads:
        copy.start()
    for read, write in zip(reads, writes):
        read.wait()
        write.start()
    for copy in writes:
        copy.wait()


def relay(arrays, pieces):
    hbm = pl.BlockSpec(memory_space=pl.ANY)
    total = sum(pieces)
    return pl.pallas_call(
        partial(relay_kernel, pieces),
        out_shape=[jax.ShapeDtypeStruct(a.shape, a.dtype) for a in arrays],
        in_specs=[hbm] * len(arrays),
        out_specs=[hbm] * len(arrays),
        scratch_shapes=[pltpu.VMEM(a.shape, a.dtype) for a in arrays]
        + [pltpu.SemaphoreType.DMA((total,)), pltpu.SemaphoreType.DMA((total,))],
        compiler_params=pltpu.CompilerParams(vmem_limit_bytes=60 * 1024 * 1024),
    )(*arrays)


def run_step(latents, cotangent, weights, momentum, step, bit):
    S = lax.axis_size("shard")
    images, HH, WW, C = latents.shape
    R = weights.shape[1]
    RP = -(-R // 64) * 64
    H = RP // 2
    LN = S // PLANE
    cells = HH * WW
    PK = H * C // 128
    dims = (S, R, RP, C, images, HH, WW)
    vmem = pl.BlockSpec(memory_space=pltpu.VMEM)
    smem = pl.BlockSpec(memory_space=pltpu.SMEM)
    hbm = pl.BlockSpec(memory_space=pl.ANY)
    V = pltpu.VMEM
    dma = pltpu.SemaphoreType.DMA
    flat = images * cells
    scratch = [
        V((flat, C), BF16),
        V((flat, C), BF16),
        V((images, cells + 2 * WW, 3 * C), BF16),
        V((images, cells + 2 * WW, 3 * C), BF16),
        V((images, C, cells), BF16),
        V((S, 2, PK, 128), BF16),
        V((3 * C, 3 * C), BF16),
        V((3 * C, 3 * C), BF16),
        V((9 * C, C), F32),
        V((S, 2, PK, 128), F32),
        V((S, PK, 128), F32),
        V((PK, 128), F32),
        V((3, LN, PK, 128), BF16),
        V((3, LN, PK, 128), BF16),
        V((LN - 1, PK, 128), BF16),
        V((LN - 1, PK, 128), BF16),
        V((2, PK, 128), F32),
        V((R, 1, C), F32),
        V((R, 1, C), F32),
        V((cells + 2 * WW, 3 * C), F32),
        V((flat, C), F32),
        dma((4 * LN + 1,)), dma((S,)),
        dma((2,)), dma((2,)),
        dma((LN,)), dma((LN,)),
        dma((3, LN)), dma((3, LN)),
        dma((LN - 1,)), dma((LN - 1,)),
        dma, dma,
        dma((2,)),
        dma((2, images)),
    ]
    flops = 6 * flat * 9 * C * C
    act, dg, nw, nm = pl.pallas_call(
        partial(step_kernel, bit, dims),
        out_shape=(
            jax.ShapeDtypeStruct((flat, C), F32),
            jax.ShapeDtypeStruct((flat, C), F32),
            jax.ShapeDtypeStruct((R, 1, C), F32),
            jax.ShapeDtypeStruct((R, 1, C), F32),
        ),
        in_specs=[hbm, hbm, vmem, vmem, smem],
        out_specs=(hbm, hbm, vmem, vmem),
        scratch_shapes=scratch,
        compiler_params=pltpu.CompilerParams(
            collective_id=bit, has_side_effects=True, vmem_limit_bytes=60 * 1024 * 1024),
        cost_estimate=pl.CostEstimate(flops=flops, bytes_accessed=12 * flat * C, transcendentals=0),
    )(latents.reshape(flat, C), cotangent.reshape(flat, C), weights.transpose(1, 0, 2), momentum.transpose(1, 0, 2), step)
    act, dg, nw, nm = relay((act, dg, nw, nm), (4, 4, 1, 1))
    return act.reshape(latents.shape), dg.reshape(latents.shape), nw.transpose(1, 0, 2), nm.transpose(1, 0, 2)


def shards(latents, cotangent, weights, momentum, step):
    bit_count = lax.axis_size("group").bit_length() - 1
    branches = [partial(run_step, bit=bit) for bit in range(bit_count)]
    args = (latents, cotangent, weights, momentum, step)
    if bit_count == 1:
        return branches[0](*args)
    return lax.switch(step[0] % bit_count, branches, *args)


def solution(mesh):
    placed = (
        P(("group", "shard"), None, None, None),
        P(("group", "shard"), None, None, None),
        P("group", "shard", None),
        P("group", "shard", None),
        P(),
    )
    return jax.shard_map(
        shards,
        mesh=mesh,
        in_specs=placed,
        out_specs=(
            P(("group", "shard"), None, None, None),
            P(("group", "shard"), None, None, None),
            P("group", "shard", None),
            P("group", "shard", None),
        ),
        check_vma=False,
    )
```

```python
from functools import partial

import jax
import jax.numpy as jnp
from jax import lax
from jax.experimental import pallas as pl
from jax.experimental.pallas import tpu as pltpu
from jax.sharding import PartitionSpec as P

beta_rate = 0.9
peak_rate = 0.1
warm_steps = 64.0
MESH = pl.DeviceIdType.MESH
F32 = jnp.float32
BF16 = jnp.bfloat16
PLANE = 4


def pack(rows):
    n, width = rows.shape
    full = width // 128
    parts = [rows[:, 128 * k:128 * (k + 1)] for k in range(full)]
    tail = rows[:, 128 * full:]
    return jnp.concatenate(parts + [jnp.concatenate([tail[:n // 2], tail[n // 2:]], 1)], 0)


def unpack(packed, n):
    full = (packed.shape[0] - n // 2) // n
    parts = [packed[n * k:n * (k + 1)] for k in range(full)]
    tail = packed[n * full:]
    return jnp.concatenate(parts + [jnp.concatenate([tail[:, :64], tail[:, 64:]], 0)], 1)


def step_kernel(bit, dims, x_hbm, c_hbm, w_ref, m_ref, step_ref,
                act_ref, dg_ref, nw_ref, nm_ref,
                x_ref, c_ref, xc, gc, xt, wg, wf, wb, g32, gb, pr, keep, sb, r1, s2, r2, tot,
                pw, pm, wide, acc,
                g_send, g_recv, e_send, e_recv, p_send, p_recv, a_send, a_recv,
                b_send, b_recv, t_send, t_recv, in_sem, out_sem):
    S, R, RP, C, images, HH, WW = dims
    H = RP // 2
    LN = S // PLANE
    cells = HH * WW
    grp = lax.axis_index("group")
    me = lax.axis_index("shard")
    q = me // PLANE
    p = me % PLANE
    px = p + 1 - 2 * (p % 2)
    py = (p + 2) % PLANE
    pd = PLANE - 1 - p
    mask = 2 ** bit
    half = (grp // mask) % 2
    mate = grp + mask - 2 * mask * half

    def shard_at(dq, col):
        return ((q + dq) % LN) * PLANE + col

    barrier = pltpu.get_barrier_semaphore()
    peers = [(grp, shard_at(dq, p)) for dq in range(1, LN)]
    peers += [(grp, shard_at(0, col)) for col in (px, py, pd)]
    peers += [(mate, me)]
    for peer in peers:
        pl.semaphore_signal(barrier, inc=1, device_id=peer, device_id_type=MESH)

    in_x = pltpu.make_async_copy(x_hbm, x_ref, in_sem.at[0])
    in_c = pltpu.make_async_copy(c_hbm, c_ref, in_sem.at[1])
    in_c.start()
    in_x.start()
    own = w_ref[:, 0, :]
    wg[me, 0] = pack(own[0:H]).astype(BF16)
    wg[me, 1] = pack(jnp.concatenate([own[H:R], jnp.zeros((RP - R, C), F32)], 0)).astype(BF16)
    pl.semaphore_wait(barrier, len(peers))

    started = []

    def send(src, dst, ss, rs, peer):
        copy = pltpu.make_async_remote_copy(src_ref=src, dst_ref=dst, send_sem=ss, recv_sem=rs,
                                            device_id=peer, device_id_type=MESH)
        copy.start()
        started.append(copy)

    def arrived(ref, sem):
        pltpu.make_async_copy(ref, ref, sem).wait()

    g_count = [0]

    def send_piece(slot, peer):
        send(wg.at[slot], wg.at[slot], g_send.at[g_count[0]], g_recv.at[slot], peer)
        g_count[0] += 1

    def wait_piece(slot):
        arrived(wg.at[slot], g_recv.at[slot])

    for dq in range(1, LN):
        send_piece(me, (grp, shard_at(dq, p)))
    x_peer = (grp, shard_at(0, px))
    y_peer = (grp, shard_at(0, py))
    send_piece(me, x_peer)
    send_piece(me, y_peer)
    send(w_ref, pw, e_send.at[0], e_recv.at[0], (mate, me))
    send(m_ref, pm, e_send.at[1], e_recv.at[1], (mate, me))

    def pass_line(dq):
        slot = shard_at(dq, p)
        wait_piece(slot)
        send_piece(slot, x_peer)
        send_piece(slot, y_peer)

    def pass_plane(dq):
        slot_x = shard_at(dq, px)
        slot_y = shard_at(dq, py)
        wait_piece(slot_x)
        wait_piece(slot_y)
        if dq % 2 == 0:
            send_piece(slot_x, y_peer)
        else:
            send_piece(slot_y, x_peer)

    CH = 8 * WW
    for buf in (xc, gc):
        for img in range(images):
            buf[img, 0:WW, :] = jnp.zeros((WW, 3 * C), BF16)
            buf[img, WW + cells:, :] = jnp.zeros((WW, 3 * C), BF16)

    def shifted(src, buf, sign):
        def body(k, _):
            img = k // (cells // CH)
            row = (k % (cells // CH)) * CH
            mid = src[pl.ds(pl.multiple_of(k * CH, CH), CH), :]
            val = mid.astype(F32)
            col = lax.broadcasted_iota(jnp.int32, (1, WW, C), 1)
            prev = pltpu.roll(val, 1, 0).reshape(CH // WW, WW, C)
            prev = jnp.where(col == 0, 0.0, prev).reshape(CH, C).astype(BF16)
            nxt = pltpu.roll(val, CH - 1, 0).reshape(CH // WW, WW, C)
            nxt = jnp.where(col == WW - 1, 0.0, nxt).reshape(CH, C).astype(BF16)
            first, last = (prev, nxt) if sign > 0 else (nxt, prev)
            dst = pl.ds(pl.multiple_of(WW + row, WW), CH)
            buf[img, dst, :] = jnp.concatenate([first, mid, last], 1)
            return 0
        lax.fori_loop(0, images * (cells // CH), body, 0)

    order = []
    for dq in range(1, LN // 2 + 1):
        order += [dq, LN - dq] if 2 * dq != LN else [dq]
    tasks = [partial(pass_line, order[0]), partial(pass_plane, 0)]
    tasks += [partial(pass_line, dq) for dq in order[1:]]
    tasks += [partial(pass_plane, dq) for dq in order]
    points = 3 * images + 1
    turn = [0]

    def pass_on():
        lo, hi = turn[0] * len(tasks) // points, (turn[0] + 1) * len(tasks) // points
        for task in tasks[lo:hi]:
            task()
        turn[0] += 1

    in_c.wait()
    shifted(c_ref, gc, -1)
    in_x.wait()
    pass_on()
    for img in range(images):
        xt[img] = x_ref[img * cells:(img + 1) * cells, :].T
        pass_on()

    def tap_rows(a):
        total = None
        for img in range(images):
            part = jnp.dot(xt[img], gc[img, WW - WW * (a - 1):WW - WW * (a - 1) + cells, :],
                           preferred_element_type=F32)
            total = part if total is None else total + part
            pass_on()
        for b in range(3):
            t = 3 * a + b
            g32[t * C:(t + 1) * C, :] = total[:, b * C:(b + 1) * C]

    def send_half(u):
        for s in range(u * PLANE, (u + 1) * PLANE):
            gb[s, 0] = pack(g32[s * R:s * R + H, :])
            gb[s, 1] = pack(jnp.concatenate([g32[s * R + H:(s + 1) * R, :], jnp.zeros((RP - R, C), F32)], 0))
        group = pl.ds(u * PLANE, PLANE)
        send(gb.at[group, 1 - half], pr.at[group], p_send.at[u], p_recv.at[u], (mate, me))

    cols = [(px, 0), (py, 1), (pd, 2)]

    def send_plane(u):
        arrived(pr.at[pl.ds(u * PLANE, PLANE)], p_recv.at[u])
        for col, k in cols:
            sb[k, u] = (gb[u * PLANE + col, half] + pr[u * PLANE + col]).astype(BF16)
            send(sb.at[k, u], r1.at[k, u], a_send.at[k, u], a_recv.at[k, u], (grp, shard_at(0, col)))

    done = 0
    sent = 0
    for a in range(3):
        tap_rows(a)
        ready = done
        while done < LN and (done + 1) * PLANE * R <= (a + 1) * 3 * C:
            send_half(done)
            done += 1
        while sent < ready:
            send_plane(sent)
            sent += 1

    shifted(x_ref, xc, 1)
    while sent < LN:
        send_plane(sent)
        sent += 1
    for dq in range(LN):
        wait_piece(shard_at(dq, pd))

    for s in range(S):
        g32[s * R:s * R + H, :] = unpack(wg[s, 0].astype(F32), H)
        g32[s * R + H:(s + 1) * R, :] = unpack(wg[s, 1].astype(F32), H)[0:R - H]
    for a in range(3):
        wf[:, a * C:(a + 1) * C] = g32[3 * a * C:3 * (a + 1) * C, :].astype(BF16)

    outs = {}

    def conv(buf, ker, out, sign, sem, img):
        wide[...] = jnp.dot(buf[img], ker[...], preferred_element_type=F32)
        val = None
        for a in range(3):
            lo = WW + sign * WW * (a - 1)
            term = wide[lo:lo + cells, a * C:(a + 1) * C]
            val = term if val is None else val + term
        rows = pl.ds(img * cells, cells)
        if img in outs:
            outs.pop(img).wait()
        acc[rows, :] = val
        outs[img] = pltpu.make_async_copy(acc.at[rows], out.at[rows], out_sem.at[sem, img])
        outs[img].start()

    def plane_sum(dq):
        u = (q + dq) % LN
        total = gb[u * PLANE + p, half] + pr[u * PLANE + p]
        for k in range(3):
            arrived(r1.at[k, u], a_recv.at[k, u])
            total = total + r1[k, u].astype(F32)
        return total

    def send_line(dq):
        s2[dq - 1] = plane_sum(dq).astype(BF16)
        send(s2.at[dq - 1], r2.at[dq - 1], b_send.at[dq - 1], b_recv.at[dq - 1], (grp, shard_at(dq, p)))

    for img in range(images):
        conv(xc, wf, act_ref, 1, 0, img)
    for b in range(3):
        wb[b * C:(b + 1) * C, :] = jnp.concatenate(
            [g32[(3 * a + b) * C:(3 * a + b + 1) * C, :].astype(BF16).T for a in range(3)], 1)
    for dq in range(1, LN):
        send_line(dq)
    keep[...] = plane_sum(0)
    for img in range(images - 1):
        conv(gc, wb, dg_ref, -1, 1, img)

    total = keep[...]
    for k in range(LN - 1):
        arrived(r2.at[k], b_recv.at[k])
        total = total + r2[k].astype(F32)
    tot[half] = total
    send(tot.at[half], tot.at[half], t_send, t_recv, (mate, me))
    conv(gc, wb, dg_ref, -1, 1, images - 1)
    arrived(pw, e_recv.at[0])
    arrived(pm, e_recv.at[1])
    arrived(tot.at[1 - half], t_recv)
    cells_group = S * images * cells
    rows = jnp.concatenate([unpack(tot[0], H), unpack(tot[1], H)[0:R - H]], 0)
    grad = rows * (0.5 * float(cells_group) ** -0.5)
    rate = peak_rate * (step_ref[0] + 1).astype(F32) / warm_steps
    moment = 0.5 * beta_rate * (m_ref[:, 0, :] + pm[:, 0, :]) + grad
    nm_ref[:, 0, :] = moment
    nw_ref[:, 0, :] = 0.5 * (w_ref[:, 0, :] + pw[:, 0, :]) - rate * moment

    for copy in started:
        copy.wait_send()
    for copy in outs.values():
        copy.wait()


def relay_kernel(pieces, *refs):
    count = (len(refs) - 2) // 3
    srcs, dsts, holds = refs[:count], refs[count:2 * count], refs[2 * count:3 * count]
    read_sem, write_sem = refs[3 * count:]
    spans = []
    for k in range(count):
        step = srcs[k].shape[0] // pieces[k]
        spans += [(k, pl.ds(i * step, step)) for i in range(pieces[k])]
    reads = [pltpu.make_async_copy(srcs[k].at[at], holds[k].at[at], read_sem.at[i])
             for i, (k, at) in enumerate(spans)]
    writes = [pltpu.make_async_copy(holds[k].at[at], dsts[k].at[at], write_sem.at[i])
              for i, (k, at) in enumerate(spans)]
    for copy in reads:
        copy.start()
    for read, write in zip(reads, writes):
        read.wait()
        write.start()
    for copy in writes:
        copy.wait()


def relay(arrays, pieces):
    hbm = pl.BlockSpec(memory_space=pl.ANY)
    total = sum(pieces)
    return pl.pallas_call(
        partial(relay_kernel, pieces),
        out_shape=[jax.ShapeDtypeStruct(a.shape, a.dtype) for a in arrays],
        in_specs=[hbm] * len(arrays),
        out_specs=[hbm] * len(arrays),
        scratch_shapes=[pltpu.VMEM(a.shape, a.dtype) for a in arrays]
        + [pltpu.SemaphoreType.DMA((total,)), pltpu.SemaphoreType.DMA((total,))],
        compiler_params=pltpu.CompilerParams(vmem_limit_bytes=60 * 1024 * 1024),
    )(*arrays)


def run_step(latents, cotangent, weights, momentum, step, bit):
    S = lax.axis_size("shard")
    images, HH, WW, C = latents.shape
    R = weights.shape[1]
    RP = -(-R // 64) * 64
    H = RP // 2
    LN = S // PLANE
    cells = HH * WW
    PK = H * C // 128
    dims = (S, R, RP, C, images, HH, WW)
    vmem = pl.BlockSpec(memory_space=pltpu.VMEM)
    smem = pl.BlockSpec(memory_space=pltpu.SMEM)
    hbm = pl.BlockSpec(memory_space=pl.ANY)
    V = pltpu.VMEM
    dma = pltpu.SemaphoreType.DMA
    flat = images * cells
    scratch = [
        V((flat, C), BF16),
        V((flat, C), BF16),
        V((images, cells + 2 * WW, 3 * C), BF16),
        V((images, cells + 2 * WW, 3 * C), BF16),
        V((images, C, cells), BF16),
        V((S, 2, PK, 128), BF16),
        V((3 * C, 3 * C), BF16),
        V((3 * C, 3 * C), BF16),
        V((9 * C, C), F32),
        V((S, 2, PK, 128), F32),
        V((S, PK, 128), F32),
        V((PK, 128), F32),
        V((3, LN, PK, 128), BF16),
        V((3, LN, PK, 128), BF16),
        V((LN - 1, PK, 128), BF16),
        V((LN - 1, PK, 128), BF16),
        V((2, PK, 128), F32),
        V((R, 1, C), F32),
        V((R, 1, C), F32),
        V((cells + 2 * WW, 3 * C), F32),
        V((flat, C), F32),
        dma((4 * LN + 1,)), dma((S,)),
        dma((2,)), dma((2,)),
        dma((LN,)), dma((LN,)),
        dma((3, LN)), dma((3, LN)),
        dma((LN - 1,)), dma((LN - 1,)),
        dma, dma,
        dma((2,)),
        dma((2, images)),
    ]
    flops = 6 * flat * 9 * C * C
    act, dg, nw, nm = pl.pallas_call(
        partial(step_kernel, bit, dims),
        out_shape=(
            jax.ShapeDtypeStruct((flat, C), F32),
            jax.ShapeDtypeStruct((flat, C), F32),
            jax.ShapeDtypeStruct((R, 1, C), F32),
            jax.ShapeDtypeStruct((R, 1, C), F32),
        ),
        in_specs=[hbm, hbm, vmem, vmem, smem],
        out_specs=(hbm, hbm, vmem, vmem),
        scratch_shapes=scratch,
        compiler_params=pltpu.CompilerParams(
            collective_id=bit, has_side_effects=True, vmem_limit_bytes=60 * 1024 * 1024),
        cost_estimate=pl.CostEstimate(flops=flops, bytes_accessed=12 * flat * C, transcendentals=0),
    )(latents.reshape(flat, C), cotangent.reshape(flat, C), weights.transpose(1, 0, 2), momentum.transpose(1, 0, 2), step)
    act, dg, nw, nm = relay((act, dg, nw, nm), (4, 4, 1, 1))
    return act.reshape(latents.shape), dg.reshape(latents.shape), nw.transpose(1, 0, 2), nm.transpose(1, 0, 2)


def shards(latents, cotangent, weights, momentum, step):
    bit_count = lax.axis_size("group").bit_length() - 1
    branches = [partial(run_step, bit=bit) for bit in range(bit_count)]
    args = (latents, cotangent, weights, momentum, step)
    if bit_count == 1:
        return branches[0](*args)
    return lax.switch(step[0] % bit_count, branches, *args)


def solution(mesh):
    placed = (
        P(("group", "shard"), None, None, None),
        P(("group", "shard"), None, None, None),
        P("group", "shard", None),
        P("group", "shard", None),
        P(),
    )
    return jax.shard_map(
        shards,
        mesh=mesh,
        in_specs=placed,
        out_specs=(
            P(("group", "shard"), None, None, None),
            P(("group", "shard"), None, None, None),
            P("group", "shard", None),
            P("group", "shard", None),
        ),
        check_vma=False,
    )
```
